32 devices in a mesh: copies: 2 (over y), tensor: 8 (over z, x), sub: 2 (over core).
Axes of the slice: x: 2, y: 2, z: 4, core: 2. Of those that a mesh axis runs over, the one named last changes fastest.
Arguments:
- acts: bfloat16 [512, 8192], P(('copies', 'sub'), 'tensor'), parts along dimension 0, may hold values from -6 to 6
- teacher_w: bfloat16 [8192, 8192], P(None, ('tensor', 'sub'))
- student_w: bfloat16 [8192, 8192], P('tensor'), may hold values from -0.09375 to 0.09375
- block_mask: int32 [64, 64], P('tensor'), may hold values from 0 to 1, as said below
Outputs:
- student_grad: float32 [16384, 8192], P(('copies', 'tensor')), parts along dimension 0
- loss: float32 [2], P('copies'), parts along dimension 0
The draws below stay inside these ranges and needn't reach their ends.
There are 2 independent parts, one for each index of `copies`. The reference program is written for one: setup_inputs(seed, part) draws one part's arguments, and reference() takes and returns one part's arrays. A program takes and returns all parts, laid end to end along the dimension named above; an argument that names none is the same for every part. Nothing has to cross between parts.
Inputs may be any that keep to these rules, and one draw needn't show every extreme that they name: `block_mask`: zeros and ones; each block row keeps its own share of blocks.
All inputs are finite; a program needn't handle non-finite values.
Results may differ from the reference program's by a relative error of at most 0.008.
Values may be sent and summed in bfloat16 or wider, within the bound.
A program may use at most 256 MiB of HBM per device.

```python
import jax
import jax.numpy as jnp

D = 8192
BLK = 128
TOKENS = 256
NBLK = 64


def draw_teacher_w(key, part):
    key = jax.random.fold_in(key, 11)
    column = jnp.arange(D, dtype=jnp.float32) / (D - 1)
    ramp = jnp.exp(jnp.log(3.0) * column)[None, :]
    base = jax.random.normal(key, (D, D), jnp.float32)
    return (base * ramp * D ** (-0.5)).astype(jnp.bfloat16)


def draw_block_mask(key, part):
    key = jax.random.fold_in(key, 7)
    first, second = jax.random.split(key)
    level = jax.random.randint(first, (NBLK, 1), 1, 16)
    values = jax.random.randint(second, (NBLK, NBLK), 0, 16)
    return (values < level).astype(jnp.int32)


def raised(drawn, key, source, target, blocks, factor):
    owner, partner = [(jnp.arange(drawn.shape[position]) // (drawn.shape[position] // blocks)).reshape([-1 if axis == position else 1 for axis in range(drawn.ndim)]) for position in (source, target)]
    chosen = jax.random.permutation(key, blocks)[partner]
    strong = (owner == chosen) | (owner == (partner + blocks // 2) % blocks)
    return jnp.where(strong, factor * drawn, drawn)


def block_scale(stream_key, shape, cuts, smallest, largest):
    loudness = 1.0
    for position, blocks in cuts:
        steps = jax.random.uniform(jax.random.fold_in(jax.random.fold_in(stream_key, 6), position), (blocks,), jnp.float32, smallest / len(cuts), largest / len(cuts))
        loudness = loudness * jnp.repeat(jnp.exp(steps), shape[position] // blocks).reshape((-1,) + (1,) * (len(shape) - 1 - position))
    return loudness


def noise(own_key, dims, width, most, shards=(), kind=jnp.bfloat16):
    gain = block_scale(own_key, dims, shards, -0.22, 0.18) if shards else 1.0
    result = jax.random.normal(own_key, dims, jnp.float32) * width * gain
    return jnp.minimum(jnp.maximum(result, -most), most).astype(kind)


def bell_draw_with(key, shape, spread, reach, shards, heavy, kind=jnp.bfloat16):
    array = spread * jax.random.normal(key, shape, jnp.float32)
    if shards:
        array = array * block_scale(key, shape, shards, -0.22, 0.18)
    return jnp.clip(raised(array, jax.random.fold_in(key, 3), *heavy), -reach, reach).astype(kind)


def setup_inputs(seed: int = 0, part: int = 0) -> dict:
    arg_keys = jax.random.split(jax.random.key(seed), 5)
    own_keys = jax.random.split(jax.random.fold_in(arg_keys[4], part), 5)
    return {
        "acts": noise(own_keys[0], (TOKENS, D), 1.0, 6.0, ((0, 2), (1, 8))),
        "teacher_w": draw_teacher_w(jax.random.fold_in(arg_keys[4], 71), part),
        "student_w": bell_draw_with(arg_keys[2], (D, D), D ** -0.5, 0.09375, ((0, 8),), (0, 1, 8, 2.0)),
        "block_mask": draw_block_mask(jax.random.fold_in(arg_keys[4], 71), part),
    }


def reference(acts, teacher_w, student_w, block_mask):
    expand = jnp.repeat(jnp.repeat(block_mask, BLK, axis=0), BLK, axis=1).astype(jnp.bfloat16)
    masked = student_w * expand
    teacher_out = jnp.dot(acts, teacher_w, preferred_element_type=jnp.float32).astype(jnp.bfloat16)
    student_out = jnp.dot(acts, masked, preferred_element_type=jnp.float32)
    teacher_f = teacher_out.astype(jnp.float32)
    difference = student_out - teacher_f
    numerator = jnp.sum(difference * difference)
    denominator = jnp.sum(teacher_f * teacher_f)
    loss = (numerator / denominator).reshape(1)
    grad_out = ((2.0 * 65536.0 / denominator) * difference).astype(jnp.bfloat16)
    gradient = jnp.dot(acts.T, grad_out, preferred_element_type=jnp.float32)
    return gradient * expand.astype(jnp.float32), loss
```

```python
import functools

import jax
import jax.numpy as jnp
from jax import lax
from jax.experimental import pallas as pl
from jax.experimental.pallas import tpu as pltpu
from jax.sharding import PartitionSpec as P

MESH = pl.DeviceIdType.MESH
F32 = jnp.float32
BF16 = jnp.bfloat16


def tensor_of(pos, n):
    high = pos // (n // 2)
    return 2 * (pos + high * (n - 1 - 2 * pos)) + high


def exchange_kernel(
    n, blk, acts_ref, tw_ref, sw_ref, mask_ref, diff_out, acts_out, stat_out,
    abuf, swbuf, twbuf, pbuf, tacc, rs_out, rs_in, dbuf, sbuf,
    in_sem, sw_sem, tw_sem, ag_send, ag_recv, sib_send, sib_recv, rs_send, rs_recv,
    dg_send, dg_recv, dsib_send, dsib_recv, out_sem,
):
    t = lax.axis_index("tensor")
    s = lax.axis_index("sub")
    z = t // 2
    x = t % 2
    r = z + x * (n - 1 - 2 * z)
    right = {"tensor": tensor_of((r + 1) % n, n)}
    left = {"tensor": tensor_of((r + n - 1) % n, n)}
    other = {"sub": 1 - s}
    rows = acts_ref.shape[0]
    half = acts_ref.shape[1] // 2
    cols = tw_ref.shape[1]
    mine = pl.ds(pl.multiple_of(s * rows, rows), rows)
    theirs = pl.ds(pl.multiple_of((1 - s) * rows, rows), rows)
    ways = (right, left)

    def source(w, k):
        return tensor_of((r + n - k) % n if w == 0 else (r + k) % n, n)

    def student_pos(w, k):
        return (r + n - 1 - k) % n if w == 0 else (r + (1 + k) % (n // 2)) % n

    def own_copy(w):
        return pltpu.make_async_copy(
            acts_ref.at[:, pl.ds(w * half, half)], abuf.at[t, w, mine], in_sem.at[w]
        )

    def sw_copy(w, k):
        col = (2 * tensor_of(student_pos(w, k), n) + s) * cols
        return pltpu.make_async_copy(
            sw_ref.at[:, pl.ds(pl.multiple_of(col, cols), cols)], swbuf.at[w, k], sw_sem.at[w, k]
        )

    def tw_copy(w, k):
        row = (2 * source(w, k) + w) * half
        return pltpu.make_async_copy(
            tw_ref.at[pl.ds(pl.multiple_of(row, half), half)], twbuf.at[w, k], tw_sem.at[w, k]
        )

    def remote(src, dst, send, recv, where):
        return pltpu.make_async_remote_copy(
            src_ref=src, dst_ref=dst, send_sem=send, recv_sem=recv,
            device_id=where, device_id_type=MESH,
        )

    def ag_copy(w, k, at):
        piece = abuf.at[source(w, at), w, mine]
        return remote(piece, piece, ag_send.at[w, k], ag_recv.at[w, k], ways[w])

    def sib_copy(w, k, whose):
        piece = abuf.at[source(w, k), w, whose]
        return remote(piece, piece, sib_send.at[w, k], sib_recv.at[w, k], other)

    def rs_copy(w, k):
        return remote(
            rs_out.at[w, k], rs_in.at[w, k], rs_send.at[w, k], rs_recv.at[w, k], ways[w]
        )

    def dg_piece(w, k, core):
        block = 2 * source(w % 2, k) + core
        return sbuf.at[block] if w == 2 else dbuf.at[block, w]

    def dg_copy(w, k, at):
        piece = dg_piece(w, at, s)
        return remote(piece, piece, dg_send.at[w, k], dg_recv.at[w, k], ways[w % 2])

    def dsib_copy(w, k, core):
        piece = dg_piece(w, k, core)
        return remote(piece, piece, dsib_send.at[w, k], dsib_recv.at[w, k], other)

    for w in range(2):
        own_copy(w).start()

    def load_student(k, c):
        sw_copy(0, k).start()
        sw_copy(1, k).start()
        return c

    def load_teacher(k, c):
        tw_copy(0, k).start()
        tw_copy(1, k).start()
        return c

    lax.fori_loop(0, n // 2, load_student, 0)
    lax.fori_loop(0, n, load_teacher, 0)

    barrier = pltpu.get_barrier_semaphore()
    for where in (right, left, other):
        pl.semaphore_signal(barrier, inc=1, device_id=where, device_id_type=MESH)
    pl.semaphore_wait(barrier, 3)

    tacc[...] = jnp.zeros_like(tacc)
    for w in range(2):
        own_copy(w).wait()

    def student(w, k):
        sw_copy(w, k).wait()
        pos = student_pos(w, k)
        first = (2 * tensor_of(pos, n) + s) * (cols // blk)
        for i in range(2 * half // blk):
            for j in range(cols // blk):
                keep = jnp.full((blk, blk), mask_ref[i, first + j].astype(F32), F32).astype(BF16)
                at = (w, k, pl.ds(i * blk, blk), pl.ds(j * blk, blk))
                swbuf[at] = swbuf[at] * keep
        total = jnp.dot(abuf[t, 0], swbuf[w, k, :half], preferred_element_type=F32)
        total += jnp.dot(abuf[t, 1], swbuf[w, k, half:], preferred_element_type=F32)
        pbuf[pos] = total

    def step(k, c):
        @pl.when(k > 0)
        def _():
            for w in range(2):
                ag_copy(w, k - 1, k).wait_recv()

        @pl.when(k < n - 1)
        def _():
            for w in range(2):
                ag_copy(w, k, k).start()

        for w in range(2):
            sib_copy(w, k, mine).start()

        @pl.when(k == 0)
        def _():
            for w in range(2):
                sib_copy(w, 0, theirs).wait_recv()

        @pl.when(k < n // 2)
        def _():
            for w in range(2):
                student(w, k)

        @pl.when(k < n - 1)
        def _():
            for w in range(2):
                pos = (r + n - 1 - k) % n if w == 0 else (r + 1 + k) % n
                part = pbuf.at[pos, pl.ds(w * rows, rows)]

                @pl.when(k == 0)
                def _():
                    rs_out[w, k] = part[...].astype(BF16)

                @pl.when(k > 0)
                def _():
                    rs_copy(w, k - 1).wait_recv()
                    rs_out[w, k] = (part[...] + rs_in[w, k - 1].astype(F32)).astype(BF16)

                rs_copy(w, k).start()

        @pl.when(k > 0)
        def _():
            for w in range(2):
                sib_copy(w, k, theirs).wait_recv()

        for w in range(2):
            tw_copy(w, k).wait()
        total = jnp.dot(abuf[source(0, k), 0], twbuf[0, k], preferred_element_type=F32)
        total += jnp.dot(abuf[source(1, k), 1], twbuf[1, k], preferred_element_type=F32)
        tacc[...] += total
        return c

    lax.fori_loop(0, n, step, 0)

    squares = []
    for w in range(2):
        rs_copy(w, n - 2).wait_recv()
        part = slice(w * rows, (w + 1) * rows)
        teacher = tacc[part].astype(BF16).astype(F32)
        difference = pbuf[r, part] + rs_in[w, n - 2].astype(F32) - teacher
        dbuf[2 * t + s, w] = difference.astype(BF16)
        squares.append((jnp.sum(difference * difference), jnp.sum(teacher * teacher)))
    index = lax.broadcasted_iota(jnp.int32, sbuf.shape[1:], 0)
    sbuf[2 * t + s] = jnp.where(
        index == 0, squares[0][0] + squares[1][0], squares[0][1] + squares[1][1]
    )

    def spread(k, c):
        @pl.when(k > 0)
        def _():
            for w in range(3):
                dg_copy(w, k - 1, k).wait_recv()

        @pl.when(k < n - 1)
        def _():
            for w in range(3):
                dg_copy(w, k, k).start()

        for w in range(3):
            dsib_copy(w, k, s).start()
        return c

    lax.fori_loop(0, n, spread, 0)

    def arrived(k, c):
        for w in range(3):
            dsib_copy(w, k, 1 - s).wait_recv()
        return c

    lax.fori_loop(0, n, arrived, 0)
    results = [
        pltpu.make_async_copy(dbuf, diff_out, out_sem.at[0]),
        pltpu.make_async_copy(abuf.at[t], acts_out, out_sem.at[1]),
        pltpu.make_async_copy(sbuf, stat_out, out_sem.at[2]),
    ]
    for copy in results:
        copy.start()

    def drain(k, c):
        for w in range(2):
            sib_copy(w, k, mine).wait_send()

            @pl.when(k < n - 1)
            def _():
                ag_copy(w, k, k).wait_send()
                rs_copy(w, k).wait_send()

        for w in range(3):
            dsib_copy(w, k, s).wait_send()

            @pl.when(k < n - 1)
            def _():
                dg_copy(w, k, k).wait_send()

        return c

    lax.fori_loop(0, n, drain, 0)
    for copy in results:
        copy.wait()


def exchange(n, acts, teacher_w, student_w, block_mask):
    rows, width = acts.shape
    half = width // 2
    cols = teacher_w.shape[1]
    blk = width // block_mask.shape[0]
    dma = pltpu.SemaphoreType.DMA
    anywhere = pl.BlockSpec(memory_space=pl.ANY)
    return pl.pallas_call(
        functools.partial(exchange_kernel, n, blk),
        out_shape=(
            jax.ShapeDtypeStruct((2 * n, 2, rows, cols), BF16),
            jax.ShapeDtypeStruct((2, 2 * rows, half), BF16),
            jax.ShapeDtypeStruct((2 * n, 8, 128), F32),
        ),
        in_specs=[anywhere] * 3 + [pl.BlockSpec(memory_space=pltpu.SMEM)],
        out_specs=(anywhere,) * 3,
        scratch_shapes=[
            pltpu.VMEM((n, 2, 2 * rows, half), BF16),
            pltpu.VMEM((2, n // 2, width, cols), BF16),
            pltpu.VMEM((2, n, half, cols), BF16),
            pltpu.VMEM((n, 2 * rows, cols), F32),
            pltpu.VMEM((2 * rows, cols), F32),
            pltpu.VMEM((2, n - 1, rows, cols), BF16),
            pltpu.VMEM((2, n - 1, rows, cols), BF16),
            pltpu.VMEM((2 * n, 2, rows, cols), BF16),
            pltpu.VMEM((2 * n, 8, 128), F32),
            dma((2,)), dma((2, n // 2)), dma((2, n)),
            dma((2, n - 1)), dma((2, n - 1)), dma((2, n)), dma((2, n)),
            dma((2, n - 1)), dma((2, n - 1)),
            dma((3, n - 1)), dma((3, n - 1)), dma((3, n)), dma((3, n)),
            dma((3,)),
        ],
        compiler_params=pltpu.CompilerParams(
            collective_id=0, has_side_effects=True, vmem_limit_bytes=50 * 2**20
        ),
        cost_estimate=pl.CostEstimate(
            flops=8 * rows * width * cols * n, bytes_accessed=4 * width * cols * n,
            transcendentals=0,
        ),
    )(acts, teacher_w, student_w, block_mask)


def gradient_kernel(blk, acts_ref, diff_ref, stat_ref, mask_ref, grad_ref, loss_ref, turned, scale):
    half = acts_ref.shape[2]
    cols = diff_ref.shape[2]
    at = pl.program_id(0)

    @pl.when(at == 0)
    def _():
        for w in range(2):
            turned[w] = acts_ref[w].astype(F32).T.astype(BF16)
        numerator = jnp.sum(stat_ref[:, 0, :]) / 128.0
        denominator = jnp.sum(stat_ref[:, 1, :]) / 128.0
        scale[0] = 2.0 * 65536.0 / denominator
        loss_ref[0] = numerator / denominator

    for w in range(2):
        value = jnp.dot(turned[w], diff_ref[0], preferred_element_type=F32)
        for i in range(half // blk):
            for j in range(cols // blk):
                row = w * (half // blk) + i
                kept = mask_ref[row, at * (cols // blk) + j].astype(F32) * scale[0]
                grad_ref[pl.ds(row * blk, blk), pl.ds(j * blk, blk)] = (
                    value[i * blk : (i + 1) * blk, j * blk : (j + 1) * blk] * kept
                )


def gradient(acts, diff, stats, block_mask):
    _, tokens, half = acts.shape
    blocks, _, cols = diff.shape
    blk = 2 * half // block_mask.shape[0]
    return pl.pallas_call(
        functools.partial(gradient_kernel, blk),
        grid=(blocks,),
        out_shape=(
            jax.ShapeDtypeStruct((2 * half, blocks * cols), F32),
            jax.ShapeDtypeStruct((1,), F32),
        ),
        in_specs=[
            pl.BlockSpec((2, tokens, half), lambda b: (0, 0, 0)),
            pl.BlockSpec((1, tokens, cols), lambda b: (b, 0, 0)),
            pl.BlockSpec(stats.shape, lambda b: (0, 0, 0)),
            pl.BlockSpec(memory_space=pltpu.SMEM),
        ],
        out_specs=(
            pl.BlockSpec((2 * half, cols), lambda b: (0, b)),
            pl.BlockSpec(memory_space=pltpu.SMEM),
        ),
        scratch_shapes=[pltpu.VMEM((2, half, tokens), BF16), pltpu.SMEM((1,), F32)],
        compiler_params=pltpu.CompilerParams(vmem_limit_bytes=40 * 2**20),
    )(acts, diff, stats, block_mask)


def ring_shards(n, acts, teacher_w, student_w, block_mask):
    diff, both, stats = exchange(n, acts, teacher_w, student_w, block_mask)
    diff = diff.reshape(diff.shape[0], -1, diff.shape[-1])
    return gradient(both, diff, stats, block_mask)


def shards(n, acts, teacher_w, student_w, block_mask):
    blk = student_w.shape[0] // block_mask.shape[0]
    expand = jnp.repeat(jnp.repeat(block_mask, blk, axis=0), blk, axis=1).astype(BF16)
    masked = student_w * expand
    s = lax.axis_index("sub")
    cols = teacher_w.shape[1]
    both = lax.all_gather(acts, "sub", axis=0, tiled=True)
    full = lax.all_gather(both, "tensor", axis=1, tiled=True)
    teacher = jnp.dot(full, teacher_w, preferred_element_type=F32).astype(BF16).astype(F32)
    own = lax.dynamic_index_in_dim(masked.reshape(-1, n, 2, cols), s, 2, keepdims=False)
    terms = jnp.dot(both, own.reshape(-1, n * cols), preferred_element_type=F32)
    student = lax.psum_scatter(terms, "tensor", scatter_dimension=1, tiled=True)
    difference = student - teacher
    numerator, denominator = lax.psum(
        (jnp.sum(difference * difference), jnp.sum(teacher * teacher)), ("tensor", "sub")
    )
    grad_out = (2.0 * 65536.0 / denominator * difference).astype(BF16)
    grad_full = lax.all_gather(grad_out, ("tensor", "sub"), axis=1, tiled=True)
    value = lax.dot_general(both, grad_full, (((0,), (0,)), ((), ())), preferred_element_type=F32)
    return value * expand.astype(F32), (numerator / denominator).reshape(1)


def solution(mesh):
    n, cores = mesh.shape["tensor"], mesh.shape["sub"]

    def run(acts, teacher_w, student_w, block_mask):
        cols = teacher_w.shape[1] // (n * cores)
        half = acts.shape[1] // n // 2
        ring = cores == 2 and 4 <= n <= 16 and n % 4 == 0 and cols % 128 == 0 and half % 128 == 0
        return jax.shard_map(
            functools.partial(ring_shards if ring else shards, n),
            mesh=mesh,
            in_specs=(
                P(("copies", "sub"), "tensor"),
                P(None, ("tensor", "sub")),
                P("tensor", None),
                P("tensor", None),
            ),
            out_specs=(P(("copies", "tensor"), None), P("copies")),
            check_vma=False,
        )(acts, teacher_w, student_w, block_mask)

    return run
```
